256 devices in a mesh: row: 8 (over x, y_hi), col: 32 (over z, y_lo, core).
Axes of the slice: x: 4, y: 4 (y_hi: 2, y_lo: 2; y = y_hi * 2 + y_lo), z: 8, core: 2. Of those that a mesh axis runs over, the one named last changes fastest.
Arguments:
- tokens: bfloat16 [512, 16384], P('col', 'row'), may hold values from -6 to 6
- gate_quant: bfloat16 [16384, 28672], P('row', 'col'), may hold values from -4 to 4
- gate_scale: float32 [128, 224], P('row', 'col'), may hold values from 0.004 to 0.016
- up_quant: bfloat16 [16384, 28672], P('row', 'col'), may hold values from -4 to 4
- up_scale: float32 [128, 224], P('row', 'col'), may hold values from 0.004 to 0.016
- down_quant: bfloat16 [28672, 16384], P('col', 'row'), may hold values from -4 to 4
- down_scale: float32 [224, 128], P('col', 'row'), may hold values from 0.003 to 0.012
Outputs:
- mixed: bfloat16 [512, 16384], P('col', 'row')
The draws below stay inside these ranges and needn't reach their ends.
All inputs are finite; a program needn't handle non-finite values.
Results may differ from the reference program's by a relative error of at most 0.0071.
Values may be sent and summed in bfloat16 or wider, within the bound.
No kernel may reach another device: no remote copies, remote signals or barrier semaphores. Data moves between devices by JAX's collectives and lax.ppermute only.
A program may use at most 64 MiB of HBM per device.

```python
import math
import jax
import jax.numpy as jnp
from jax import lax

D = 16384
FF = 28672
BLOCK = 128
ROWS = 512
N_COL = 32


def block_scale(rng, shape, split, low, largest):
    def one(axis_at, parts):
        draws = jax.random.uniform(jax.random.fold_in(jax.random.fold_in(rng, 6), axis_at), (parts,), jnp.float32, low / len(split), largest / len(split))
        return jnp.repeat(jnp.exp(draws), shape[axis_at] // parts).reshape((-1,) + (1,) * (len(shape) - axis_at - 1))

    factor_of = one(*split[0])
    for cut in split[1:]:
        factor_of = factor_of * one(*cut)
    return factor_of


def bell_draw(rng, dims, spread, bound, cuts=(), kind=jnp.bfloat16):
    array = spread * jax.random.normal(rng, dims, jnp.float32)
    if cuts:
        array = array * block_scale(rng, dims, cuts, -0.22, 0.18)
    return jnp.clip(array, -bound, bound).astype(kind)


def setup_inputs(seed: int = 0) -> dict:
    keys = jax.random.split(jax.random.key(seed), 8)
    tokens = bell_draw(keys[0], (ROWS, D), 1.0, 6.0, ((0, 32), (1, 8)))
    gate_quant = bell_draw(keys[1], (D, FF), 1.0, 4.0, ((0, 8), (1, 32)))
    gate_scale = jnp.clip(jnp.exp(math.log(0.016) - 1.3862944 * jax.random.uniform(keys[2], (D // BLOCK, FF // BLOCK), jnp.float32) ** block_scale(keys[2], (D // BLOCK, FF // BLOCK), ((0, 8), (1, 32)), -0.2, 0.2)), 0.004, 0.016)
    up_quant = bell_draw(keys[3], (D, FF), 1.0, 4.0, ((0, 8), (1, 32)))
    up_scale = jnp.clip(jnp.exp(math.log(0.016) - 1.3862944 * jax.random.uniform(keys[4], (D // BLOCK, FF // BLOCK), jnp.float32) ** block_scale(keys[4], (D // BLOCK, FF // BLOCK), ((0, 8), (1, 32)), -0.2, 0.2)), 0.004, 0.016)
    down_quant = bell_draw(keys[5], (FF, D), 1.0, 4.0, ((0, 32), (1, 8)))
    down_scale = jnp.clip(jnp.exp(math.log(0.012) - 1.3862944 * jax.random.uniform(keys[6], (FF // BLOCK, D // BLOCK), jnp.float32) ** block_scale(keys[6], (FF // BLOCK, D // BLOCK), ((0, 32), (1, 8)), -0.2, 0.2)), 0.003, 0.012)
    return dict(tokens=tokens, gate_quant=gate_quant, gate_scale=gate_scale, up_quant=up_quant, up_scale=up_scale, down_quant=down_quant, down_scale=down_scale)


def dequant(quant, scale):
    height, width = quant.shape
    blocks = quant.astype(jnp.float32).reshape(height // BLOCK, BLOCK, width // BLOCK, BLOCK)
    return (blocks * scale[:, None, :, None]).reshape(height, width).astype(jnp.bfloat16)


def reference(tokens, gate_quant, gate_scale, up_quant, up_scale, down_quant, down_scale):
    slab_width = FF // N_COL
    slab_blocks = slab_width // BLOCK
    slab_count = FF // slab_width

    def hidden_slab(index):
        offset = index * slab_width
        block_offset = index * slab_blocks
        gate_weight = dequant(lax.dynamic_slice_in_dim(gate_quant, offset, slab_width, 1),
                              lax.dynamic_slice_in_dim(gate_scale, block_offset, slab_blocks, 1))
        up_weight = dequant(lax.dynamic_slice_in_dim(up_quant, offset, slab_width, 1),
                            lax.dynamic_slice_in_dim(up_scale, block_offset, slab_blocks, 1))
        gate = jnp.dot(tokens, gate_weight, preferred_element_type=jnp.float32)
        upward = jnp.dot(tokens, up_weight, preferred_element_type=jnp.float32)
        return (jax.nn.silu(gate) * upward).astype(jnp.bfloat16)

    def down_step(total, index):
        offset = index * slab_width
        block_offset = index * slab_blocks
        hidden = hidden_slab(index)
        down_weight = dequant(lax.dynamic_slice_in_dim(down_quant, offset, slab_width, 0),
                              lax.dynamic_slice_in_dim(down_scale, block_offset, slab_blocks, 0))
        return total + jnp.dot(hidden, down_weight, preferred_element_type=jnp.float32), None

    start_total = jnp.zeros((tokens.shape[0], tokens.shape[1]), jnp.float32)
    total, unused = lax.scan(down_step, start_total, jnp.arange(slab_count, dtype=jnp.int32))
    return total.astype(jnp.bfloat16)
```

```python
import jax
import jax.numpy as jnp
from jax import lax
from jax.experimental import pallas as pl
from jax.experimental.pallas import tpu as pltpu
from jax.sharding import Mesh, PartitionSpec as P

BLOCK = 128
COL = ("z", "yl", "core")
ROW = ("x", "yh")
LIMIT = 48 * 1024 * 1024


def shift(value, axis, count, by):
    return lax.ppermute(value, axis, [(i, (i + by) % count) for i in range(count)])


def dequant(quant, scale):
    parts = []
    for i in range(quant.shape[0] // BLOCK):
        rows = quant[i * BLOCK : (i + 1) * BLOCK, :].astype(jnp.float32)
        parts.append((rows * scale(i)).astype(jnp.bfloat16))
    return jnp.concatenate(parts, axis=0)


def gate_up_kernel(me, gate_scale, up_scale, *refs):
    pieces, gate, up = refs[:4], refs[4], refs[5]
    outs, features = refs[6:14], refs[14]
    step = pl.program_id(0)

    @pl.when(step == 0)
    def _():
        for chunk in range(8):
            slot = lax.rem(chunk + 8 - me[0], 8)
            rows = pieces[chunk // 2][64 * (chunk % 2) : 64 * (chunk % 2 + 1), :]
            features[pl.ds(pl.multiple_of(slot * 64, 64), 64), :] = rows

    weight = jnp.concatenate(
        [
            dequant(gate[...], lambda i: gate_scale[i, step]),
            dequant(up[...], lambda i: up_scale[i, step]),
        ],
        axis=1,
    )
    total = jnp.dot(features[...], weight, preferred_element_type=jnp.float32)
    for k, out in enumerate(outs):
        out[...] = total[64 * k : 64 * (k + 1)].astype(jnp.bfloat16)


def gate_up(me, pieces, gate, gate_scale, up, up_scale):
    depth, width = gate.shape
    whole = pl.BlockSpec((128, depth), lambda j, *_: (0, 0))
    column = pl.BlockSpec((depth, BLOCK), lambda j, *_: (0, j))
    return pl.pallas_call(
        gate_up_kernel,
        grid_spec=pltpu.PrefetchScalarGridSpec(
            num_scalar_prefetch=3,
            grid=(width // BLOCK,),
            in_specs=[whole] * 4 + [column] * 2,
            out_specs=[pl.BlockSpec((64, 2 * BLOCK), lambda j, *_: (0, j))] * 8,
            scratch_shapes=[pltpu.VMEM((512, depth), jnp.bfloat16)],
        ),
        out_shape=[jax.ShapeDtypeStruct((64, 2 * width), jnp.bfloat16)] * 8,
        compiler_params=pltpu.CompilerParams(vmem_limit_bytes=LIMIT),
        cost_estimate=pl.CostEstimate(
            flops=2 * 512 * depth * 2 * width, bytes_accessed=12 * 1024 * 1024, transcendentals=0
        ),
        name="gate_up",
    )(me, gate_scale, up_scale, *pieces, gate, up)


def silu_kernel(*refs):
    parts, out = refs[:-1], refs[-1]
    for j in range(out.shape[1] // BLOCK):
        at = slice(2 * j * BLOCK, 2 * (j + 1) * BLOCK)
        total = parts[0][:, at].astype(jnp.float32)
        for part in parts[1:]:
            total = total + part[:, at].astype(jnp.float32)
        gate, up = total[:, :BLOCK], total[:, BLOCK:]
        out[:, j * BLOCK : (j + 1) * BLOCK] = (gate / (1.0 + jnp.exp(-gate)) * up).astype(jnp.bfloat16)


def hidden_of(parts):
    rows, width = parts[0].shape
    return pl.pallas_call(
        silu_kernel,
        out_shape=jax.ShapeDtypeStruct((rows, width // 2), jnp.bfloat16),
        compiler_params=pltpu.CompilerParams(vmem_limit_bytes=LIMIT),
        name="hidden",
    )(*parts)


def down_kernel(me, scale, *refs):
    pieces, quant = refs[:8], refs[8]
    keep, send, hidden = refs[9:12]
    step = pl.program_id(0)

    @pl.when(step == 0)
    def _():
        for k, piece in enumerate(pieces):
            chunk = lax.rem(me[0] + 8 - k, 8)
            hidden[pl.ds(pl.multiple_of(chunk * 64, 64), 64), :] = piece[...]

    weight = jnp.concatenate(
        [
            dequant(quant[:, :BLOCK], lambda i: scale[i, 2 * step]),
            dequant(quant[:, BLOCK:], lambda i: scale[i, 2 * step + 1]),
        ],
        axis=1,
    )
    total = jnp.dot(hidden[...], weight, preferred_element_type=jnp.float32)
    keep[...] = total[:256].astype(jnp.bfloat16)
    send[...] = total[256:].astype(jnp.bfloat16)


def down(me, pieces, quant, scale):
    depth, width = quant.shape
    whole = pl.BlockSpec((64, depth), lambda j, *_: (0, 0))
    out = pl.BlockSpec((256, 2 * BLOCK), lambda j, *_: (0, j))
    return pl.pallas_call(
        down_kernel,
        grid_spec=pltpu.PrefetchScalarGridSpec(
            num_scalar_prefetch=2,
            grid=(width // (2 * BLOCK),),
            in_specs=[whole] * 8 + [pl.BlockSpec((depth, 2 * BLOCK), lambda j, *_: (0, j))],
            out_specs=[out] * 2,
            scratch_shapes=[pltpu.VMEM((512, depth), jnp.bfloat16)],
        ),
        out_shape=[jax.ShapeDtypeStruct((256, width), jnp.bfloat16)] * 2,
        compiler_params=pltpu.CompilerParams(vmem_limit_bytes=LIMIT),
        cost_estimate=pl.CostEstimate(
            flops=2 * 512 * depth * width, bytes_accessed=7 * 1024 * 1024, transcendentals=0
        ),
        name="down",
    )(me, scale, *pieces, quant)


def add(a, b):
    return (a.astype(jnp.float32) + b.astype(jnp.float32)).astype(jnp.bfloat16)


def local(tokens, gate_quant, gate_scale, up_quant, up_scale, down_quant, down_scale):
    me = (lax.axis_index("x") * 2 + lax.axis_index("yh")).astype(jnp.int32).reshape(1)
    own = jnp.concatenate([tokens] + [shift(tokens, "z", 8, k) for k in range(1, 8)], axis=0)
    own_core = shift(own, "core", 2, 1)
    other = shift(own, "yl", 2, 1)
    other_core = shift(other, "core", 2, 1)
    sums = gate_up(me, [own, other, own_core, other_core], gate_quant, gate_scale, up_quant, up_scale)
    hidden = hidden_of([sums[0]] + [shift(sums[k], ROW, 8, k) for k in range(1, 8)])
    pieces = [hidden] + [shift(hidden, ROW, 8, k) for k in range(1, 8)]
    keep, send = down(me, pieces, down_quant, down_scale)
    got = shift(send, "core", 2, 1)
    near = add(keep[:128], got[:128])
    far = add(keep[128:], got[128:])
    total = add(near, shift(far, "yl", 2, 1))
    mixed = total[:16].astype(jnp.float32)
    for k in range(1, 8):
        mixed = mixed + shift(total[16 * k : 16 * (k + 1)], "z", 8, -k).astype(jnp.float32)
    return mixed.astype(jnp.bfloat16)


def solution(mesh):
    fine = Mesh(mesh.devices.reshape(4, 2, 8, 2, 2), ROW + COL)
    placed = (
        P(COL, ROW),
        P(ROW, COL),
        P(ROW, COL),
        P(ROW, COL),
        P(ROW, COL),
        P(COL, ROW),
        P(COL, ROW),
    )
    return jax.shard_map(
        local, mesh=fine, in_specs=placed, out_specs=P(COL, ROW), check_vma=False
    )
```

```python
import jax
import jax.numpy as jnp
from jax import lax
from jax.experimental import pallas as pl
from jax.experimental.pallas import tpu as pltpu
from jax.sharding import Mesh, PartitionSpec as P

BLOCK = 128
WIDE = 256
COL = ("z", "yl", "core")
ROW = ("x", "yh")
LIMIT = 24 * 1024 * 1024
F32 = jnp.float32
BF16 = jnp.bfloat16


def swap(value, axis):
    return lax.ppermute(value, axis, [(0, 1), (1, 0)])


def shift_x(value, by):
    return lax.ppermute(value, "x", [(i, (i + by) % 4) for i in range(4)])


def shift_z(value, by):
    pairs = []
    for z in range(8):
        pairs.append((2 * z, 2 * ((z + by) % 8)))
        pairs.append((2 * z + 1, 2 * ((z - by) % 8) + 1))
    return lax.ppermute(value, ("z", "core"), pairs)


def call(name, body, outs, ins, scalars=(), later=(), scratch=(), limit=LIMIT // 2):
    counts = [len(scalars), len(ins), len(later), len(outs)]

    def kernel(*refs):
        groups, at = [], 0
        for count in counts:
            groups.append(refs[at : at + count])
            at += count
        numbers, inputs, _, results = groups
        body(numbers, inputs, results, refs[at:])

    vmem = pl.BlockSpec(memory_space=pltpu.VMEM)
    return pl.pallas_call(
        kernel,
        in_specs=[pl.BlockSpec(memory_space=pltpu.SMEM)] * counts[0]
        + [vmem] * counts[1]
        + [pl.BlockSpec(memory_space=pl.ANY)] * counts[2],
        out_specs=[vmem] * counts[3],
        out_shape=[jax.ShapeDtypeStruct(shape, dtype) for shape, dtype in outs],
        scratch_shapes=list(scratch),
        compiler_params=pltpu.CompilerParams(vmem_limit_bytes=limit),
        cost_estimate=pl.CostEstimate(flops=1024, bytes_accessed=1024, transcendentals=0),
        name=name,
    )(*scalars, *ins, *later)


def columns(j, width):
    return pl.ds(pl.multiple_of(j * width, width), width)


def down_weight(quant, scale):
    depth, width = quant.shape

    def body(scales, quants, outs, _):
        def step(i, carry):
            rows = pl.ds(pl.multiple_of(i * BLOCK, BLOCK), BLOCK)
            for j in range(width // BLOCK):
                at = slice(j * BLOCK, (j + 1) * BLOCK)
                block = quants[0][rows, at].astype(F32)
                outs[0][rows, at] = (block * scales[0][j, i]).astype(BF16)
            return carry

        lax.fori_loop(0, depth // BLOCK, step, 0)

    outs = [((depth, width), BF16)]
    return call("down_weight", body, outs, [quant], scalars=[scale.T], limit=LIMIT)[0]


def joined(parts, later=()):
    def body(_, ins, outs, __):
        at = 0
        for part in ins:
            outs[0][at : at + part.shape[0], :] = part[...]
            at += part.shape[0]

    shape = (sum(part.shape[0] for part in parts), parts[0].shape[1])
    return call("joined", body, [(shape, BF16)], parts, later=later)[0]


def gate_up(me, pieces, gate, gate_scale, up, up_scale, later=()):
    depth, width = gate.shape
    count = 2 * width // WIDE

    def body(numbers, ins, outs, scratch):
        features, held = scratch
        quants, scales = ins[2:], numbers[1:]

        def fill(j):
            for side in range(2):
                for i in range(depth // BLOCK):
                    rows = slice(i * BLOCK, (i + 1) * BLOCK)
                    block = quants[side][rows, j * BLOCK : (j + 1) * BLOCK].astype(F32)
                    block = (block * scales[side][j, i]).astype(BF16)
                    held[j % 2, rows, side * BLOCK : (side + 1) * BLOCK] = block

        for chunk in range(4):
            at = pl.multiple_of(lax.rem(chunk + 4 - numbers[0][0], 4) * 64, 64)
            rows = slice(64 * (chunk % 2), 64 * (chunk % 2 + 1))
            features[pl.ds(at, 64), :] = ins[chunk // 2][rows, :]
        fill(0)
        for j in range(count):
            if j + 1 < count:
                fill(j + 1)
            total = jnp.dot(features[...], held[j % 2], preferred_element_type=F32)
            for k, out in enumerate(outs):
                out[:, j * WIDE : (j + 1) * WIDE] = total[64 * k : 64 * (k + 1)].astype(BF16)

    return call(
        "gate_up",
        body,
        [((64, 2 * width), BF16)] * 4,
        [*pieces, gate, up],
        scalars=[me, gate_scale.T, up_scale.T],
        later=later,
        scratch=[pltpu.VMEM((256, depth), BF16), pltpu.VMEM((2, depth, WIDE), BF16)],
        limit=LIMIT,
    )


def sum_x(outs, arrived, later=()):
    def body(_, ins, results, __):
        total = ins[0][...].astype(F32)
        for part in ins[1:]:
            total = total + part[...].astype(F32)
        results[0][...] = total
        results[1][...] = total.astype(BF16)

    shape = outs[0].shape
    return call("sum_x", body, [(shape, F32), (shape, BF16)], [outs[0], *arrived], later=later)


def silu(own, other, out):
    for j in range(out.shape[1] // BLOCK):
        at = slice(j * WIDE, (j + 1) * WIDE)
        total = own[:, at] + other[:, at].astype(F32)
        gate, up = total[:, :BLOCK], total[:, BLOCK:]
        hidden = gate / (1.0 + jnp.exp(-gate)) * up
        out[:, j * BLOCK : (j + 1) * BLOCK] = hidden.astype(BF16)


def hidden_and_sum(own, other, outs, arrived):
    rows, width = own.shape

    def body(_, ins, results, __):
        silu(ins[-2], ins[-1], results[0])
        total = ins[0][...].astype(F32)
        for part in ins[1:-2]:
            total = total + part[...].astype(F32)
        results[1][...] = total
        results[2][...] = total.astype(BF16)

    results = [((rows, width // 2), BF16), ((rows, width), F32), ((rows, width), BF16)]
    return call("hidden_and_sum", body, results, [outs[0], *arrived, own, other])


def hidden_of(own, other, later=()):
    rows, width = own.shape

    def body(_, ins, outs, __):
        silu(ins[0], ins[1], outs[0])

    return call("hidden", body, [((rows, width // 2), BF16)], [own, other], later=later)[0]


def down(me, pieces, weight, later=()):
    depth, width = weight.shape

    def body(numbers, ins, outs, scratch):
        hidden = scratch[0]
        for k in range(4):
            at = pl.multiple_of(lax.rem(numbers[0][0] + 4 - k, 4) * 64, 64)
            hidden[pl.ds(at, 64), :] = ins[k][...]

        def step(j, carry):
            at = columns(j, WIDE)
            total = jnp.dot(hidden[...], ins[4][:, at], preferred_element_type=F32)
            outs[0][:, at] = total[:128]
            outs[1][:, at] = total[128:].astype(BF16)
            return carry

        lax.fori_loop(0, width // WIDE, step, 0)

    return call(
        "down",
        body,
        [((128, width), F32), ((128, width), BF16)],
        [*pieces, weight],
        scalars=[me],
        later=later,
        scratch=[pltpu.VMEM((256, depth), BF16)],
    )


def sum_far(near, got):
    def body(_, ins, outs, __):
        total = (ins[0][...] + ins[1][...].astype(F32)).astype(BF16)
        outs[0][...] = total[:80]
        outs[1][...] = total[80:]

    width = near.shape[1]
    return call("sum_far", body, [((80, width), BF16), ((48, width), BF16)], [near, got])


def sum_near(near, got, other, low, parts):
    def body(_, ins, outs, __):
        at = 0
        for out in outs:
            rows = slice(low + at, low + at + out.shape[0])
            total = ins[0][rows] + ins[1][rows].astype(F32)
            total = total + ins[2][at : at + out.shape[0]].astype(F32)
            out[...] = total.astype(out.dtype)
            at += out.shape[0]

    outs = [((rows, near.shape[1]), kind) for rows, kind in parts]
    return call("sum_near", body, outs, [near, got, other])


def relay(own, arrived):
    def body(_, ins, outs, __):
        outs[0][:16] = (ins[0][:16] + ins[1][32:].astype(F32)).astype(BF16)
        outs[0][16:] = ins[0][16:].astype(BF16)

    return call("relay", body, [(own.shape, BF16)], [own, arrived])[0]


def sum_z(own, third, second, first):
    def body(_, ins, outs, __):
        total = ins[1][:32].astype(F32) + ins[2][...].astype(F32) + ins[3][...].astype(F32)
        outs[0][...] = ins[0][...] + total[:16]
        outs[1][...] = total[16:]

    return call("sum_z", body, [(own.shape, F32)] * 2, [own, third, second, first])


def spread_x(value):
    x1, x3, x2 = (shift_x(value, k) for k in (1, 3, 2))
    return [value, x1, x2, x3]


def local(tokens, gate_quant, gate_scale, up_quant, up_scale, down_quant, down_scale):
    me = lax.axis_index("x").astype(jnp.int32).reshape(1)
    both = (gate_quant, gate_scale, up_quant, up_scale)
    last_weight = down_weight(down_quant, down_scale)

    chip = joined([tokens, swap(tokens, "core")])
    z4 = shift_z(tokens, 4)
    z3, z2, z1 = (shift_z(chip, j) for j in (3, 2, 1))
    a = joined([tokens, z1, z2, z3, z4])
    b, c = swap(a, "core"), swap(a, "yl")

    outs_a = gate_up(me, [a, b], *both)
    parts_a = [shift_x(outs_a[k], k) for k in (2, 1, 3)]
    c = joined([c], later=[outs_a[0]])
    outs_c = gate_up(me, [c, swap(c, "core")], *both)
    total_a, sent_a = sum_x(outs_a, parts_a, later=[outs_c[0]])
    other_a = swap(sent_a, "yh")
    parts_c = [shift_x(outs_c[k], k) for k in (2, 1, 3)]
    hidden_a, total_c, sent_c = hidden_and_sum(total_a, other_a, outs_c, parts_c)
    gathered_a = spread_x(hidden_a)
    hidden_c = hidden_of(total_c, swap(sent_c, "yh"))
    gathered_c = spread_x(hidden_c)
    near_a, far_a = down(me, gathered_a, last_weight)
    near_c, far_c = down(me, gathered_c, last_weight, later=[far_a])

    sent2, sent1 = sum_far(near_c, swap(far_c, "core"))
    got = swap(far_a, "core")
    other1, other2 = swap(sent1, "yl"), swap(sent2, "yl")
    third = shift_z(sum_near(near_a, got, other1, 80, [(48, BF16)])[0], -3)
    parts = [(16, F32), (32, F32), (32, BF16)]
    own, first, second = sum_near(near_a, got, other2, 0, parts)
    second = shift_z(second, -2)
    first = shift_z(relay(first, third), -1)
    keep, send = sum_z(own, third, second, first)
    return (keep + swap(send, "core")).astype(BF16)


def solution(mesh):
    fine = Mesh(mesh.devices.reshape(4, 2, 8, 2, 2), ROW + COL)
    placed = (
        P(COL, ROW),
        P(ROW, COL),
        P(ROW, COL),
        P(ROW, COL),
        P(ROW, COL),
        P(COL, ROW),
        P(COL, ROW),
    )
    return jax.shard_map(
        local, mesh=fine, in_specs=placed, out_specs=P(COL, ROW), check_vma=False
    )
```

```python
import jax
import jax.numpy as jnp
from jax import lax
from jax.experimental import pallas as pl
from jax.experimental.pallas import tpu as pltpu
from jax.sharding import Mesh, PartitionSpec as P

BLOCK = 128
WIDE = 256
COL = ("z", "yl", "core")
ROW = ("x", "yh")
LIMIT = 24 * 1024 * 1024
F32 = jnp.float32
BF16 = jnp.bfloat16


def swap(value, axis):
    return lax.ppermute(value, axis, [(0, 1), (1, 0)])


def shift_x(value, by):
    return lax.ppermute(value, "x", [(i, (i + by) % 4) for i in range(4)])


def shift_z(value, by):
    pairs = []
    for z in range(8):
        pairs.append((2 * z, 2 * ((z + by) % 8)))
        pairs.append((2 * z + 1, 2 * ((z - by) % 8) + 1))
    return lax.ppermute(value, ("z", "core"), pairs)


def call(name, body, outs, ins, scalars=(), later=(), scratch=(), limit=LIMIT // 2):
    counts = [len(scalars), len(ins), len(later), len(outs)]

    def kernel(*refs):
        groups, at = [], 0
        for count in counts:
            groups.append(refs[at : at + count])
            at += count
        numbers, inputs, _, results = groups
        body(numbers, inputs, results, refs[at:])

    vmem = pl.BlockSpec(memory_space=pltpu.VMEM)
    return pl.pallas_call(
        kernel,
        in_specs=[pl.BlockSpec(memory_space=pltpu.SMEM)] * counts[0]
        + [vmem] * counts[1]
        + [pl.BlockSpec(memory_space=pl.ANY)] * counts[2],
        out_specs=[vmem] * counts[3],
        out_shape=[jax.ShapeDtypeStruct(shape, dtype) for shape, dtype in outs],
        scratch_shapes=list(scratch),
        compiler_params=pltpu.CompilerParams(vmem_limit_bytes=limit),
        cost_estimate=pl.CostEstimate(flops=1024, bytes_accessed=1024, transcendentals=0),
        name=name,
    )(*scalars, *ins, *later)


def columns(j, width):
    return pl.ds(pl.multiple_of(j * width, width), width)


def down_weight(quant, scale):
    depth, width = quant.shape

    def body(scales, quants, outs, _):
        def step(i, carry):
            rows = pl.ds(pl.multiple_of(i * BLOCK, BLOCK), BLOCK)
            for j in range(width // BLOCK):
                at = slice(j * BLOCK, (j + 1) * BLOCK)
                block = quants[0][rows, at].astype(F32)
                outs[0][rows, at] = (block * scales[0][j, i]).astype(BF16)
            return carry

        lax.fori_loop(0, depth // BLOCK, step, 0)

    outs = [((depth, width), BF16)]
    return call("down_weight", body, outs, [quant], scalars=[scale.T], limit=LIMIT)[0]


def joined(parts, later=()):
    def body(_, ins, outs, __):
        at = 0
        for part in ins:
            outs[0][at : at + part.shape[0], :] = part[...]
            at += part.shape[0]

    shape = (sum(part.shape[0] for part in parts), parts[0].shape[1])
    return call("joined", body, [(shape, BF16)], parts, later=later)[0]


def gate_up(me, pieces, gate, gate_scale, up, up_scale, later=()):
    depth, width = gate.shape
    count = 2 * width // WIDE

    def body(numbers, ins, outs, scratch):
        features, held = scratch
        quants, scales = ins[-2:], numbers[1:]

        def fill(j):
            for side in range(2):
                for i in range(depth // BLOCK):
                    rows = slice(i * BLOCK, (i + 1) * BLOCK)
                    block = quants[side][rows, j * BLOCK : (j + 1) * BLOCK].astype(F32)
                    block = (block * scales[side][j, i]).astype(BF16)
                    held[j % 2, rows, side * BLOCK : (side + 1) * BLOCK] = block

        row = 0
        for piece in ins[:-2]:
            for low in range(0, piece.shape[0], 16):
                slot = lax.rem(row // 64 + 4 - numbers[0][0], 4)
                at = pl.multiple_of(slot * 64 + row % 64, 16)
                features[pl.ds(at, 16), :] = piece[low : low + 16, :]
                row += 16
        fill(0)
        for j in range(count):
            if j + 1 < count:
                fill(j + 1)
            total = jnp.dot(features[...], held[j % 2], preferred_element_type=F32)
            for k, out in enumerate(outs):
                out[:, j * WIDE : (j + 1) * WIDE] = total[64 * k : 64 * (k + 1)].astype(BF16)

    return call(
        "gate_up",
        body,
        [((64, 2 * width), BF16)] * 4,
        [*pieces, gate, up],
        scalars=[me, gate_scale.T, up_scale.T],
        later=later,
        scratch=[pltpu.VMEM((256, depth), BF16), pltpu.VMEM((2, depth, WIDE), BF16)],
        limit=LIMIT,
    )


def sum_x(outs, arrived, later=()):
    def body(_, ins, results, __):
        total = ins[0][...].astype(F32)
        for part in ins[1:]:
            total = total + part[...].astype(F32)
        results[0][...] = total
        results[1][...] = total.astype(BF16)

    shape = outs[0].shape
    return call("sum_x", body, [(shape, F32), (shape, BF16)], [outs[0], *arrived], later=later)


def silu(own, other, out):
    for j in range(out.shape[1] // BLOCK):
        at = slice(j * WIDE, (j + 1) * WIDE)
        total = own[:, at] + other[:, at].astype(F32)
        gate, up = total[:, :BLOCK], total[:, BLOCK:]
        hidden = gate / (1.0 + jnp.exp(-gate)) * up
        out[:, j * BLOCK : (j + 1) * BLOCK] = hidden.astype(BF16)


def hidden_and_sum(own, other, outs, arrived):
    rows, width = own.shape

    def body(_, ins, results, __):
        silu(ins[-2], ins[-1], results[0])
        total = ins[0][...].astype(F32)
        for part in ins[1:-2]:
            total = total + part[...].astype(F32)
        results[1][...] = total
        results[2][...] = total.astype(BF16)

    results = [((rows, width // 2), BF16), ((rows, width), F32), ((rows, width), BF16)]
    return call("hidden_and_sum", body, results, [outs[0], *arrived, own, other])


def hidden_of(own, other, later=()):
    rows, width = own.shape

    def body(_, ins, outs, __):
        silu(ins[0], ins[1], outs[0])

    return call("hidden", body, [((rows, width // 2), BF16)], [own, other], later=later)[0]


def down(me, pieces, weight, later=()):
    depth, width = weight.shape

    def body(numbers, ins, outs, scratch):
        hidden = scratch[0]
        for k in range(4):
            at = pl.multiple_of(lax.rem(numbers[0][0] + 4 - k, 4) * 64, 64)
            hidden[pl.ds(at, 64), :] = ins[k][...]

        def step(j, carry):
            at = columns(j, WIDE)
            total = jnp.dot(hidden[...], ins[4][:, at], preferred_element_type=F32)
            outs[0][:, at] = total[:128]
            outs[1][:, at] = total[128:].astype(BF16)
            return carry

        lax.fori_loop(0, width // WIDE, step, 0)

    return call(
        "down",
        body,
        [((128, width), F32), ((128, width), BF16)],
        [*pieces, weight],
        scalars=[me],
        later=later,
        scratch=[pltpu.VMEM((256, depth), BF16)],
    )


def sum_far(near, got):
    def body(_, ins, outs, __):
        total = (ins[0][...] + ins[1][...].astype(F32)).astype(BF16)
        outs[0][...] = total[:80]
        outs[1][...] = total[80:]

    width = near.shape[1]
    return call("sum_far", body, [((80, width), BF16), ((48, width), BF16)], [near, got])


def sum_near(near, got, other, low, parts):
    def body(_, ins, outs, __):
        at = 0
        for out in outs:
            rows = slice(low + at, low + at + out.shape[0])
            total = ins[0][rows] + ins[1][rows].astype(F32)
            total = total + ins[2][at : at + out.shape[0]].astype(F32)
            out[...] = total.astype(out.dtype)
            at += out.shape[0]

    outs = [((rows, near.shape[1]), kind) for rows, kind in parts]
    return call("sum_near", body, outs, [near, got, other])


def relay(own, arrived):
    def body(_, ins, outs, __):
        outs[0][:16] = (ins[0][:16] + ins[1][32:].astype(F32)).astype(BF16)
        outs[0][16:] = ins[0][16:].astype(BF16)

    return call("relay", body, [(own.shape, BF16)], [own, arrived])[0]


def sum_z(own, third, second, first):
    def body(_, ins, outs, __):
        total = ins[1][:32].astype(F32) + ins[2][...].astype(F32) + ins[3][...].astype(F32)
        outs[0][...] = ins[0][...] + total[:16]
        outs[1][...] = total[16:]

    return call("sum_z", body, [(own.shape, F32)] * 2, [own, third, second, first])


def spread_x(value):
    x1, x3, x2 = (shift_x(value, k) for k in (1, 3, 2))
    return [value, x1, x2, x3]


def local(tokens, gate_quant, gate_scale, up_quant, up_scale, down_quant, down_scale):
    me = lax.axis_index("x").astype(jnp.int32).reshape(1)
    both = (gate_quant, gate_scale, up_quant, up_scale)
    last_weight = down_weight(down_quant, down_scale)

    chip = jnp.concatenate([tokens, swap(tokens, "core")])
    z4 = shift_z(tokens, 4)
    z3, z2, z1 = (shift_z(chip, j) for j in (3, 2, 1))
    a1, a2 = jnp.concatenate([tokens, z1]), jnp.concatenate([z2, z3, z4])
    c1, c2 = swap(a1, "yl"), swap(a2, "yl")
    b1, b2 = swap(a1, "core"), swap(a2, "core")

    outs_a = gate_up(me, [a1, a2, b1, b2], *both)
    parts_a = [shift_x(outs_a[k], k) for k in (2, 1, 3)]
    c1, c2 = joined([c1], later=[outs_a[0]]), joined([c2], later=[outs_a[0]])
    outs_c = gate_up(me, [c1, c2, swap(c1, "core"), swap(c2, "core")], *both)
    total_a, sent_a = sum_x(outs_a, parts_a, later=[outs_c[0]])
    other_a = swap(sent_a, "yh")
    parts_c = [shift_x(outs_c[k], k) for k in (2, 1, 3)]
    hidden_a, total_c, sent_c = hidden_and_sum(total_a, other_a, outs_c, parts_c)
    gathered_a = spread_x(hidden_a)
    hidden_c = hidden_of(total_c, swap(sent_c, "yh"))
    gathered_c = spread_x(hidden_c)
    near_a, far_a = down(me, gathered_a, last_weight)
    near_c, far_c = down(me, gathered_c, last_weight, later=[far_a])

    sent2, sent1 = sum_far(near_c, swap(far_c, "core"))
    got = swap(far_a, "core")
    other1, other2 = swap(sent1, "yl"), swap(sent2, "yl")
    third = shift_z(sum_near(near_a, got, other1, 80, [(48, BF16)])[0], -3)
    parts = [(16, F32), (32, F32), (32, BF16)]
    own, first, second = sum_near(near_a, got, other2, 0, parts)
    second = shift_z(second, -2)
    first = shift_z(relay(first, third), -1)
    keep, send = sum_z(own, third, second, first)
    return (keep + swap(send, "core")).astype(BF16)


def solution(mesh):
    fine = Mesh(mesh.devices.reshape(4, 2, 8, 2, 2), ROW + COL)
    placed = (
        P(COL, ROW),
        P(ROW, COL),
        P(ROW, COL),
        P(ROW, COL),
        P(ROW, COL),
        P(COL, ROW),
        P(COL, ROW),
    )
    return jax.shard_map(
        local, mesh=fine, in_specs=placed, out_specs=P(COL, ROW), check_vma=False
    )
```

```python
import jax
import jax.numpy as jnp
from jax import lax
from jax.experimental import pallas as pl
from jax.experimental.pallas import tpu as pltpu
from jax.sharding import Mesh, PartitionSpec as P

BLOCK = 128
WIDE = 256
COL = ("z", "yl", "core")
ROW = ("x", "yh")
LIMIT = 24 * 1024 * 1024
F32 = jnp.float32
BF16 = jnp.bfloat16


def swap(value, axis):
    return lax.ppermute(value, axis, [(0, 1), (1, 0)])


def shift_x(value, by):
    return lax.ppermute(value, "x", [(i, (i + by) % 4) for i in range(4)])


def shift_z(value, by):
    pairs = []
    for z in range(8):
        pairs.append((2 * z, 2 * ((z + by) % 8)))
        pairs.append((2 * z + 1, 2 * ((z - by) % 8) + 1))
    return lax.ppermute(value, ("z", "core"), pairs)


def call(name, body, outs, ins, scalars=(), later=(), scratch=(), limit=LIMIT // 2):
    counts = [len(scalars), len(ins), len(later), len(outs)]

    def kernel(*refs):
        groups, at = [], 0
        for count in counts:
            groups.append(refs[at : at + count])
            at += count
        numbers, inputs, _, results = groups
        body(numbers, inputs, results, refs[at:])

    vmem = pl.BlockSpec(memory_space=pltpu.VMEM)
    return pl.pallas_call(
        kernel,
        in_specs=[pl.BlockSpec(memory_space=pltpu.SMEM)] * counts[0]
        + [vmem] * counts[1]
        + [pl.BlockSpec(memory_space=pl.ANY)] * counts[2],
        out_specs=[vmem] * counts[3],
        out_shape=[jax.ShapeDtypeStruct(shape, dtype) for shape, dtype in outs],
        scratch_shapes=list(scratch),
        compiler_params=pltpu.CompilerParams(vmem_limit_bytes=limit),
        cost_estimate=pl.CostEstimate(flops=1024, bytes_accessed=1024, transcendentals=0),
        name=name,
    )(*scalars, *ins, *later)


def columns(j, width):
    return pl.ds(pl.multiple_of(j * width, width), width)


def down_weight(quant, scale):
    depth, width = quant.shape

    def body(scales, quants, outs, _):
        def step(i, carry):
            rows = pl.ds(pl.multiple_of(i * BLOCK, BLOCK), BLOCK)
            for j in range(width // BLOCK):
                at = slice(j * BLOCK, (j + 1) * BLOCK)
                block = quants[0][rows, at].astype(F32)
                outs[0][rows, at] = (block * scales[0][j, i]).astype(BF16)
            return carry

        lax.fori_loop(0, depth // BLOCK, step, 0)

    outs = [((depth, width), BF16)]
    return call("down_weight", body, outs, [quant], scalars=[scale.T], limit=LIMIT)[0]


def joined(parts, later=()):
    def body(_, ins, outs, __):
        at = 0
        for part in ins:
            outs[0][at : at + part.shape[0], :] = part[...]
            at += part.shape[0]

    shape = (sum(part.shape[0] for part in parts), parts[0].shape[1])
    return call("joined", body, [(shape, BF16)], parts, later=later)[0]


def gate_up(me, pieces, gate, up, scale, later=()):
    depth, width = gate.shape
    count = 2 * width // WIDE

    def body(numbers, ins, outs, scratch):
        features, held = scratch
        quants, scale = ins[-2:], numbers[1]

        def fill(j):
            for side in range(2):
                for i in range(depth // BLOCK):
                    rows = slice(i * BLOCK, (i + 1) * BLOCK)
                    block = quants[side][rows, j * BLOCK : (j + 1) * BLOCK].astype(F32)
                    block = (block * scale[side * count + j, i]).astype(BF16)
                    held[j % 2, rows, side * BLOCK : (side + 1) * BLOCK] = block

        row = 0
        for piece in ins[:-2]:
            for low in range(0, piece.shape[0], 16):
                slot = lax.rem(row // 64 + 4 - numbers[0][0], 4)
                at = pl.multiple_of(slot * 64 + row % 64, 16)
                features[pl.ds(at, 16), :] = piece[low : low + 16, :]
                row += 16
        fill(0)
        for j in range(count):
            if j + 1 < count:
                fill(j + 1)
            total = jnp.dot(features[...], held[j % 2], preferred_element_type=F32)
            for k, out in enumerate(outs):
                out[:, j * WIDE : (j + 1) * WIDE] = total[64 * k : 64 * (k + 1)].astype(BF16)

    return call(
        "gate_up",
        body,
        [((64, 2 * width), BF16)] * 4,
        [*pieces, gate, up],
        scalars=[me, scale],
        later=later,
        scratch=[pltpu.VMEM((256, depth), BF16), pltpu.VMEM((2, depth, WIDE), BF16)],
        limit=LIMIT,
    )


def sum_x(outs, arrived, later=()):
    def body(_, ins, results, __):
        total = ins[0][...].astype(F32)
        for part in ins[1:]:
            total = total + part[...].astype(F32)
        results[0][...] = total
        results[1][...] = total.astype(BF16)

    shape = outs[0].shape
    return call("sum_x", body, [(shape, F32), (shape, BF16)], [outs[0], *arrived], later=later)


def silu(own, other, out):
    for j in range(out.shape[1] // BLOCK):
        at = slice(j * WIDE, (j + 1) * WIDE)
        total = own[:, at] + other[:, at].astype(F32)
        gate, up = total[:, :BLOCK], total[:, BLOCK:]
        hidden = gate / (1.0 + jnp.exp(-gate)) * up
        out[:, j * BLOCK : (j + 1) * BLOCK] = hidden.astype(BF16)


def hidden_and_sum(own, other, outs, arrived):
    rows, width = own.shape

    def body(_, ins, results, __):
        silu(ins[-2], ins[-1], results[0])
        total = ins[0][...].astype(F32)
        for part in ins[1:-2]:
            total = total + part[...].astype(F32)
        results[1][...] = total
        results[2][...] = total.astype(BF16)

    results = [((rows, width // 2), BF16), ((rows, width), F32), ((rows, width), BF16)]
    return call("hidden_and_sum", body, results, [outs[0], *arrived, own, other])


def hidden_of(own, other, later=()):
    rows, width = own.shape

    def body(_, ins, outs, __):
        silu(ins[0], ins[1], outs[0])

    return call("hidden", body, [((rows, width // 2), BF16)], [own, other], later=later)[0]


def down(me, pieces, weight, later=()):
    depth, width = weight.shape

    def body(numbers, ins, outs, scratch):
        hidden = scratch[0]
        for k in range(4):
            at = pl.multiple_of(lax.rem(numbers[0][0] + 4 - k, 4) * 64, 64)
            hidden[pl.ds(at, 64), :] = ins[k][...]

        def step(j, carry):
            at = columns(j, WIDE)
            total = jnp.dot(hidden[...], ins[4][:, at], preferred_element_type=F32)
            outs[0][:, at] = total[:128]
            outs[1][:, at] = total[128:].astype(BF16)
            return carry

        lax.fori_loop(0, width // WIDE, step, 0)

    return call(
        "down",
        body,
        [((128, width), F32), ((128, width), BF16)],
        [*pieces, weight],
        scalars=[me],
        later=later,
        scratch=[pltpu.VMEM((256, depth), BF16)],
    )


def sum_far(near, got):
    def body(_, ins, outs, __):
        total = (ins[0][...] + ins[1][...].astype(F32)).astype(BF16)
        outs[0][...] = total[:80]
        outs[1][...] = total[80:]

    width = near.shape[1]
    return call("sum_far", body, [((80, width), BF16), ((48, width), BF16)], [near, got])


def sum_near(near, got, other, low, parts):
    def body(_, ins, outs, __):
        at = 0
        for out in outs:
            rows = slice(low + at, low + at + out.shape[0])
            total = ins[0][rows] + ins[1][rows].astype(F32)
            total = total + ins[2][at : at + out.shape[0]].astype(F32)
            out[...] = total.astype(out.dtype)
            at += out.shape[0]

    outs = [((rows, near.shape[1]), kind) for rows, kind in parts]
    return call("sum_near", body, outs, [near, got, other])


def relay(own, arrived):
    def body(_, ins, outs, __):
        outs[0][:16] = (ins[0][:16] + ins[1][32:].astype(F32)).astype(BF16)
        outs[0][16:] = ins[0][16:].astype(BF16)

    return call("relay", body, [(own.shape, BF16)], [own, arrived])[0]


def sum_z(own, third, second, first):
    def body(_, ins, outs, __):
        total = ins[1][:32].astype(F32) + ins[2][...].astype(F32) + ins[3][...].astype(F32)
        outs[0][...] = ins[0][...] + total[:16]
        outs[1][...] = total[16:]

    return call("sum_z", body, [(own.shape, F32)] * 2, [own, third, second, first])


def spread_x(value):
    x1, x3, x2 = (shift_x(value, k) for k in (1, 3, 2))
    return [value, x1, x2, x3]


def local(tokens, gate_quant, gate_scale, up_quant, up_scale, down_quant, down_scale):
    me = lax.axis_index("x").astype(jnp.int32).reshape(1)
    both = (gate_quant, up_quant, jnp.concatenate([gate_scale.T, up_scale.T]))
    last_weight = down_weight(down_quant, down_scale)

    chip = jnp.concatenate([tokens, swap(tokens, "core")])
    z4 = shift_z(tokens, 4)
    z3, z2, z1 = (shift_z(chip, j) for j in (3, 2, 1))
    a1, a2 = jnp.concatenate([tokens, z1]), jnp.concatenate([z2, z3, z4])
    c1, c2 = swap(a1, "yl"), swap(a2, "yl")
    b1, b2 = swap(a1, "core"), swap(a2, "core")

    outs_a = gate_up(me, [a1, a2, b1, b2], *both)
    parts_a = [shift_x(outs_a[k], k) for k in (1, 3, 2)]
    c1, c2 = joined([c1], later=[outs_a[0]]), joined([c2], later=[outs_a[0]])
    outs_c = gate_up(me, [c1, c2, swap(c1, "core"), swap(c2, "core")], *both)
    total_a, sent_a = sum_x(outs_a, parts_a, later=[outs_c[0]])
    other_a = swap(sent_a, "yh")
    parts_c = [shift_x(outs_c[k], k) for k in (1, 3, 2)]
    hidden_a, total_c, sent_c = hidden_and_sum(total_a, other_a, outs_c, parts_c)
    gathered_a = spread_x(hidden_a)
    hidden_c = hidden_of(total_c, swap(sent_c, "yh"))
    gathered_c = spread_x(hidden_c)
    near_a, far_a = down(me, gathered_a, last_weight)
    near_c, far_c = down(me, gathered_c, last_weight, later=[far_a])

    sent2, sent1 = sum_far(near_c, swap(far_c, "core"))
    got = swap(far_a, "core")
    other1, other2 = swap(sent1, "yl"), swap(sent2, "yl")
    third = shift_z(sum_near(near_a, got, other1, 80, [(48, BF16)])[0], -3)
    parts = [(16, F32), (32, F32), (32, BF16)]
    own, first, second = sum_near(near_a, got, other2, 0, parts)
    second = shift_z(second, -2)
    first = shift_z(relay(first, third), -1)
    keep, send = sum_z(own, third, second, first)
    return (keep + swap(send, "core")).astype(BF16)


def solution(mesh):
    fine = Mesh(mesh.devices.reshape(4, 2, 8, 2, 2), ROW + COL)
    placed = (
        P(COL, ROW),
        P(ROW, COL),
        P(ROW, COL),
        P(ROW, COL),
        P(ROW, COL),
        P(COL, ROW),
        P(COL, ROW),
    )
    return jax.shard_map(
        local, mesh=fine, in_specs=placed, out_specs=P(COL, ROW), check_vma=False
    )
```

```python
import jax
import jax.numpy as jnp
from jax import lax
from jax.experimental import pallas as pl
from jax.experimental.pallas import tpu as pltpu
from jax.sharding import Mesh, PartitionSpec as P

BLOCK = 128
WIDE = 256
COL = ("z", "yl", "core")
ROW = ("x", "yh")
LIMIT = 24 * 1024 * 1024
F32 = jnp.float32
BF16 = jnp.bfloat16


def swap(value, axis):
    return lax.ppermute(value, axis, [(0, 1), (1, 0)])


def shift_x(value, by):
    return lax.ppermute(value, "x", [(i, (i + by) % 4) for i in range(4)])


def shift_z(value, by):
    pairs = []
    for z in range(8):
        pairs.append((2 * z, 2 * ((z + by) % 8)))
        pairs.append((2 * z + 1, 2 * ((z - by) % 8) + 1))
    return lax.ppermute(value, ("z", "core"), pairs)


def call(name, body, outs, ins, scalars=(), later=(), scratch=(), limit=LIMIT // 2):
    counts = [len(scalars), len(ins), len(later), len(outs)]

    def kernel(*refs):
        groups, at = [], 0
        for count in counts:
            groups.append(refs[at : at + count])
            at += count
        numbers, inputs, _, results = groups
        body(numbers, inputs, results, refs[at:])

    vmem = pl.BlockSpec(memory_space=pltpu.VMEM)
    return pl.pallas_call(
        kernel,
        in_specs=[pl.BlockSpec(memory_space=pltpu.SMEM)] * counts[0]
        + [vmem] * counts[1]
        + [pl.BlockSpec(memory_space=pl.ANY)] * counts[2],
        out_specs=[vmem] * counts[3],
        out_shape=[jax.ShapeDtypeStruct(shape, dtype) for shape, dtype in outs],
        scratch_shapes=list(scratch),
        compiler_params=pltpu.CompilerParams(vmem_limit_bytes=limit),
        cost_estimate=pl.CostEstimate(flops=1024, bytes_accessed=1024, transcendentals=0),
        name=name,
    )(*scalars, *ins, *later)


def columns(j, width):
    return pl.ds(pl.multiple_of(j * width, width), width)


def down_weight(quant, scale):
    depth, width = quant.shape

    def body(scales, quants, outs, _):
        def step(i, carry):
            rows = pl.ds(pl.multiple_of(i * BLOCK, BLOCK), BLOCK)
            for j in range(width // BLOCK):
                at = slice(j * BLOCK, (j + 1) * BLOCK)
                block = quants[0][rows, at].astype(F32)
                outs[0][rows, at] = (block * scales[0][j, i]).astype(BF16)
            return carry

        lax.fori_loop(0, depth // BLOCK, step, 0)

    outs = [((depth, width), BF16)]
    return call("down_weight", body, outs, [quant], scalars=[scale.T], limit=LIMIT)[0]


def joined(parts, later=()):
    def body(_, ins, outs, __):
        at = 0
        for part in ins:
            outs[0][at : at + part.shape[0], :] = part[...]
            at += part.shape[0]

    shape = (sum(part.shape[0] for part in parts), parts[0].shape[1])
    return call("joined", body, [(shape, BF16)], parts, later=later)[0]


def gate_up(me, pieces, gate, up, scale, later=()):
    depth, width = gate.shape
    count = 2 * width // WIDE

    def body(numbers, ins, outs, scratch):
        features, held = scratch
        quants, scale = ins[-2:], numbers[1]

        def fill(j):
            for side in range(2):
                for i in range(depth // BLOCK):
                    rows = slice(i * BLOCK, (i + 1) * BLOCK)
                    block = quants[side][rows, j * BLOCK : (j + 1) * BLOCK].astype(F32)
                    block = (block * scale[side * count + j, i]).astype(BF16)
                    held[j % 2, rows, side * BLOCK : (side + 1) * BLOCK] = block

        row = 0
        for piece in ins[:-2]:
            for low in range(0, piece.shape[0], 16):
                slot = lax.rem(row // 64 + 4 - numbers[0][0], 4)
                at = pl.multiple_of(slot * 64 + row % 64, 16)
                features[pl.ds(at, 16), :] = piece[low : low + 16, :]
                row += 16
        fill(0)
        for j in range(count):
            if j + 1 < count:
                fill(j + 1)
            total = jnp.dot(features[...], held[j % 2], preferred_element_type=F32)
            for k, out in enumerate(outs):
                out[:, j * WIDE : (j + 1) * WIDE] = total[64 * k : 64 * (k + 1)].astype(BF16)

    return call(
        "gate_up",
        body,
        [((64, 2 * width), BF16)] * 4,
        [*pieces, gate, up],
        scalars=[me, scale],
        later=later,
        scratch=[pltpu.VMEM((256, depth), BF16), pltpu.VMEM((2, depth, WIDE), BF16)],
        limit=LIMIT,
    )


def sum_x(outs, arrived, later=()):
    def body(_, ins, results, __):
        total = ins[0][...].astype(F32)
        for part in ins[1:]:
            total = total + part[...].astype(F32)
        results[0][...] = total
        results[1][...] = total.astype(BF16)

    shape = outs[0].shape
    return call("sum_x", body, [(shape, F32), (shape, BF16)], [outs[0], *arrived], later=later)


def silu(own, other, out):
    for j in range(out.shape[1] // BLOCK):
        at = slice(j * WIDE, (j + 1) * WIDE)
        total = own[:, at] + other[:, at].astype(F32)
        gate, up = total[:, :BLOCK], total[:, BLOCK:]
        hidden = gate / (1.0 + jnp.exp(-gate)) * up
        out[:, j * BLOCK : (j + 1) * BLOCK] = hidden.astype(BF16)


def hidden_and_sum(own, other, outs, arrived):
    rows, width = own.shape

    def body(_, ins, results, __):
        silu(ins[-2], ins[-1], results[0])
        total = ins[0][...].astype(F32)
        for part in ins[1:-2]:
            total = total + part[...].astype(F32)
        results[1][...] = total
        results[2][...] = total.astype(BF16)

    results = [((rows, width // 2), BF16), ((rows, width), F32), ((rows, width), BF16)]
    return call("hidden_and_sum", body, results, [outs[0], *arrived, own, other])


def hidden_of(own, other, later=()):
    rows, width = own.shape

    def body(_, ins, outs, __):
        silu(ins[0], ins[1], outs[0])

    return call("hidden", body, [((rows, width // 2), BF16)], [own, other], later=later)[0]


def down(me, pieces, weight, cut=128, later=()):
    depth, width = weight.shape

    def body(numbers, ins, outs, scratch):
        hidden = scratch[0]
        for k in range(4):
            at = pl.multiple_of(lax.rem(numbers[0][0] + 4 - k, 4) * 64, 64)
            hidden[pl.ds(at, 64), :] = ins[k][...]

        def step(j, carry):
            at = columns(j, WIDE)
            total = jnp.dot(hidden[...], ins[4][:, at], preferred_element_type=F32)
            outs[0][:, at] = total[:128]
            outs[1][:, at] = total[128 : 128 + cut].astype(BF16)
            if cut < 128:
                outs[2][:, at] = total[128 + cut :].astype(BF16)
            return carry

        lax.fori_loop(0, width // WIDE, step, 0)

    return call(
        "down",
        body,
        [((128, width), F32), ((cut, width), BF16)]
        + [((128 - cut, width), BF16)] * (cut < 128),
        [*pieces, weight],
        scalars=[me],
        later=later,
        scratch=[pltpu.VMEM((256, depth), BF16)],
    )


def sum_far(near, got, low):
    def body(_, ins, outs, __):
        rows = slice(low, low + ins[1].shape[0])
        outs[0][...] = (ins[0][rows] + ins[1][...].astype(F32)).astype(BF16)

    return call("sum_far", body, [(got.shape, BF16)], [near, got])[0]


def sum_near(near, got, other, low, parts):
    def body(_, ins, outs, __):
        at = 0
        for out in outs:
            rows = slice(low + at, low + at + out.shape[0])
            total = ins[0][rows] + ins[1][rows].astype(F32)
            total = total + ins[2][at : at + out.shape[0]].astype(F32)
            out[...] = total.astype(out.dtype)
            at += out.shape[0]

    outs = [((rows, near.shape[1]), kind) for rows, kind in parts]
    return call("sum_near", body, outs, [near, got, other])


def relay(own, arrived):
    def body(_, ins, outs, __):
        outs[0][:16] = (ins[0][:16] + ins[1][32:].astype(F32)).astype(BF16)
        outs[0][16:] = ins[0][16:].astype(BF16)

    return call("relay", body, [(own.shape, BF16)], [own, arrived])[0]


def sum_z(own, third, second, first):
    def body(_, ins, outs, __):
        total = ins[1][:32].astype(F32) + ins[2][...].astype(F32) + ins[3][...].astype(F32)
        outs[0][...] = ins[0][...] + total[:16]
        outs[1][...] = total[16:]

    return call("sum_z", body, [(own.shape, F32)] * 2, [own, third, second, first])


def spread_x(value):
    x1, x3, x2 = (shift_x(value, k) for k in (1, 3, 2))
    return [value, x1, x2, x3]


def local(tokens, gate_quant, gate_scale, up_quant, up_scale, down_quant, down_scale):
    me = lax.axis_index("x").astype(jnp.int32).reshape(1)
    both = (gate_quant, up_quant, jnp.concatenate([gate_scale.T, up_scale.T]))
    last_weight = down_weight(down_quant, down_scale)

    chip = jnp.concatenate([tokens, swap(tokens, "core")])
    z4 = shift_z(tokens, 4)
    z3, z2, z1 = (shift_z(chip, j) for j in (3, 2, 1))
    a1, a2 = jnp.concatenate([tokens, z1]), jnp.concatenate([z2, z3, z4])
    c1, c2 = swap(a1, "yl"), swap(a2, "yl")
    b1, b2 = swap(a1, "core"), swap(a2, "core")

    outs_a = gate_up(me, [a1, a2, b1, b2], *both)
    parts_a = [shift_x(outs_a[k], k) for k in (1, 3, 2)]
    c1, c2 = joined([c1], later=[outs_a[0]]), joined([c2], later=[outs_a[0]])
    outs_c = gate_up(me, [c1, c2, swap(c1, "core"), swap(c2, "core")], *both)
    total_a, sent_a = sum_x(outs_a, parts_a, later=[outs_c[0]])
    other_a = swap(sent_a, "yh")
    parts_c = [shift_x(outs_c[k], k) for k in (1, 3, 2)]
    hidden_a, total_c, sent_c = hidden_and_sum(total_a, other_a, outs_c, parts_c)
    gathered_a = spread_x(hidden_a)
    hidden_c = hidden_of(total_c, swap(sent_c, "yh"))
    gathered_c = spread_x(hidden_c)
    near_a, far_a = down(me, gathered_a, last_weight)
    near_c, far2, far1 = down(me, gathered_c, last_weight, cut=80, later=[far_a])

    sent1 = sum_far(near_c, swap(far1, "core"), 80)
    sent2 = sum_far(near_c, swap(far2, "core"), 0)
    got = swap(far_a, "core")
    other1, other2 = swap(sent1, "yl"), swap(sent2, "yl")
    third = shift_z(sum_near(near_a, got, other1, 80, [(48, BF16)])[0], -3)
    parts = [(16, F32), (32, F32), (32, BF16)]
    own, first, second = sum_near(near_a, got, other2, 0, parts)
    second = shift_z(second, -2)
    first = shift_z(relay(first, third), -1)
    keep, send = sum_z(own, third, second, first)
    return (keep + swap(send, "core")).astype(BF16)


def solution(mesh):
    fine = Mesh(mesh.devices.reshape(4, 2, 8, 2, 2), ROW + COL)
    placed = (
        P(COL, ROW),
        P(ROW, COL),
        P(ROW, COL),
        P(ROW, COL),
        P(ROW, COL),
        P(COL, ROW),
        P(COL, ROW),
    )
    return jax.shard_map(
        local, mesh=fine, in_specs=placed, out_specs=P(COL, ROW), check_vma=False
    )
```
